32 devices in a mesh: ctx: 16 (over z, y, core), head: 2 (over x).
Axes of the slice: x: 2, y: 2, z: 4, core: 2. Of those that a mesh axis runs over, the one named last changes fastest.
Arguments:
- q_nope: bfloat16 [1024, 8192], P('ctx', 'head'), may hold values from -6 to 6
- query_rope: bfloat16 [1024, 4096], P('ctx', 'head'), may hold values from -80 to 80
- latent: bfloat16 [1024, 512], P('ctx'), may hold values from -6 to 6
- key_rope: bfloat16 [1024, 64], P('ctx'), may hold values from -3 to 3
- w_uk: bfloat16 [64, 128, 512], P('head'), may hold values from -0.5 to 0.5
- w_uv: bfloat16 [64, 512, 128], P('head'), may hold values from -1 to 1
- w_out: bfloat16 [64, 128, 3584], P('head', None, 'ctx'), may hold values from -0.0625 to 0.0625
Outputs:
- mixed: bfloat16 [1024, 3584], P(('ctx', 'head'))
The draws below stay inside these ranges and needn't reach their ends.
All inputs are finite; a program needn't handle non-finite values.
Results may differ from the reference program's by a relative error of at most 0.015.
Values may be sent and summed in bfloat16 or wider, within the bound.
A program may use at most 128 MiB of HBM per device.

```python
import jax
import jax.numpy as jnp
from jax import lax

TOK_DEV = 64
HEADS = 64
NOPE = 128
ROPE = 64
LAT = 512
VD = 128
D_OUT = 3584
TOKENS = 1024
N_CTX = 16


def draw_key_rope(key, part):
    key = jax.random.fold_in(key, 11)
    values = jnp.clip(jax.random.normal(key, (TOKENS, ROPE), jnp.float32), -3.0, 3.0)
    return values.astype(jnp.bfloat16)


def draw_query_rope(key, part):
    key = jax.random.fold_in(key, 23)
    first_key = jax.random.fold_in(key, 0)
    values = jnp.clip(jax.random.normal(first_key, (TOKENS, HEADS, ROPE), jnp.float32), -3.0, 3.0)
    return values.reshape(TOKENS, HEADS * ROPE).astype(jnp.bfloat16)


def steps_of(key, shape, pieces, smallest, largest):
    loudness = 1.0
    for axis_at, blocks in pieces:
        steps = jax.random.uniform(jax.random.fold_in(jax.random.fold_in(key, 6), axis_at), (blocks,), jnp.float32, smallest / len(pieces), largest / len(pieces))
        loudness = loudness * jnp.repeat(jnp.exp(steps), shape[axis_at] // blocks).reshape((-1,) + (1,) * (len(shape) - 1 - axis_at))
    return loudness


def gaussian(rng, dims, width, most, cuts=(), held_as=jnp.bfloat16):
    array = width * jax.random.normal(rng, dims, jnp.float32)
    if cuts:
        array = array * steps_of(rng, dims, cuts, -0.22, 0.18)
    return jnp.clip(array, -most, most).astype(held_as)


def setup_inputs(seed: int = 0) -> dict:
    arg_keys = jax.random.split(jax.random.key(seed), 8)
    return {
        "q_nope": gaussian(arg_keys[0], (TOKENS, HEADS * NOPE), 1.0, 6.0, ((0, 16), (1, 2))),
        "query_rope": draw_query_rope(jax.random.fold_in(arg_keys[7], 71), 0),
        "latent": gaussian(arg_keys[2], (TOKENS, LAT), 1.0, 6.0, ((0, 16),)),
        "key_rope": draw_key_rope(jax.random.fold_in(arg_keys[7], 71), 0),
        "w_uk": gaussian(arg_keys[4], (HEADS, NOPE, LAT), NOPE ** -0.5, 0.5, ((0, 2),)),
        "w_uv": gaussian(arg_keys[5], (HEADS, LAT, VD), (LAT // 16) ** -0.5, 1.0, ((0, 2),)),
        "w_out": gaussian(arg_keys[6], (HEADS, VD, D_OUT), (HEADS * VD) ** -0.5, 0.0625, ((0, 2), (2, 16))),
    }


def positions(total_rows):
    row_ids = jnp.arange(total_rows, dtype=jnp.int32)
    half_len = TOK_DEV // 2
    block_index = row_ids // TOK_DEV
    within_block = row_ids % TOK_DEV
    return jnp.where(within_block < half_len, block_index * half_len + within_block, (2 * N_CTX - 1 - block_index) * half_len + within_block - half_len)


def reference(q_nope, query_rope, latent, key_rope, w_uk, w_uv, w_out):
    score_scale = (NOPE + ROPE) ** -0.5
    order = positions(TOKENS)
    visible = order[None, :] <= order[:, None]
    nope_heads = q_nope.reshape(TOKENS, HEADS, NOPE).transpose(1, 0, 2)
    rope_heads = query_rope.reshape(TOKENS, HEADS, ROPE).transpose(1, 0, 2)

    def one_head(head_items):
        nope_part, rope_part, absorb, expand = head_items
        query_latent = jnp.dot(nope_part, absorb, preferred_element_type=jnp.float32).astype(jnp.bfloat16)
        scores = jnp.dot(query_latent, latent.T, preferred_element_type=jnp.float32) + jnp.dot(rope_part, key_rope.T, preferred_element_type=jnp.float32)
        scores = jnp.where(visible, scores * score_scale, -jnp.inf)
        probs = jax.nn.softmax(scores, axis=1).astype(jnp.bfloat16)
        latent_out = jnp.dot(probs, latent, preferred_element_type=jnp.float32).astype(jnp.bfloat16)
        return jnp.dot(latent_out, expand, preferred_element_type=jnp.float32).astype(jnp.bfloat16)

    head_out = lax.map(one_head, (nope_heads, rope_heads, w_uk, w_uv))
    flat_out = head_out.transpose(1, 0, 2).reshape(TOKENS, HEADS * VD)
    return jnp.dot(flat_out, w_out.reshape(HEADS * VD, D_OUT), preferred_element_type=jnp.float32).astype(jnp.bfloat16)
```

```python
import jax
import jax.numpy as jnp
from jax import lax
from jax.sharding import PartitionSpec as P

NOPE = 128
ROPE = 64


def folded_position(row_ids, shard_rows, shard_count):
    half_len = shard_rows // 2
    block_index = row_ids // shard_rows
    within_block = row_ids % shard_rows
    return jnp.where(
        within_block < half_len,
        block_index * half_len + within_block,
        (2 * shard_count - 1 - block_index) * half_len + within_block - half_len,
    )


def attend_block(
    state_now, lat_block, rope_block, pos_block, query_latent, query_rope, query_pos, score_scale
):
    best_now, total_now, accum_now = state_now
    scores = jnp.einsum(
        "qhl,kl->qhk", query_latent, lat_block, preferred_element_type=jnp.float32
    ) + jnp.einsum("qhr,kr->qhk", query_rope, rope_block, preferred_element_type=jnp.float32)
    scores = scores * score_scale
    visible = pos_block[None, None, :] <= query_pos[:, None, None]
    block_best = jnp.max(jnp.where(visible, scores, -jnp.inf), axis=2)
    best_next = jnp.maximum(best_now, block_best)
    weights = jnp.where(visible, jnp.exp(scores - best_next[:, :, None]), 0.0)
    factor = jnp.exp(best_now - best_next)
    total_next = total_now * factor + jnp.sum(weights, axis=2)
    accum_next = accum_now * factor[:, :, None] + jnp.einsum(
        "qhk,kl->qhl", weights.astype(jnp.bfloat16), lat_block, preferred_element_type=jnp.float32
    )
    return (best_next, total_next, accum_next)


def make_fold(query_latent, query_rope, query_pos, row_map, score_scale):

    def fold_keys(state_now, key_piece, row_start):
        lat_piece, rope_piece = key_piece
        key_count = lat_piece.shape[0]
        block_len = key_count
        while block_len > 512 and block_len % 2 == 0:
            block_len = block_len // 2
        blocks = key_count // block_len
        key_pos = row_map(jnp.arange(key_count, dtype=jnp.int32))

        def scan_step(state_inner, block_items):
            lat_block, rope_block, pos_block = block_items
            return (
                attend_block(
                    state_inner,
                    lat_block,
                    rope_block,
                    pos_block,
                    query_latent,
                    query_rope,
                    query_pos,
                    score_scale,
                ),
                None,
            )

        state_out, unused = lax.scan(
            scan_step,
            state_now,
            (
                lat_piece.reshape(blocks, block_len, lat_piece.shape[1]),
                rope_piece.reshape(blocks, block_len, rope_piece.shape[1]),
                key_pos.reshape(blocks, block_len),
            ),
        )
        return state_out

    return fold_keys


def shards(q_nope, query_rope, latent, key_rope, w_uk, w_uv, w_out):
    shard_rows = latent.shape[0]
    shard_count = lax.axis_size("ctx")
    heads_here = w_uk.shape[0]
    score_scale = (NOPE + ROPE) ** (-0.5)
    nope_part = q_nope.reshape(shard_rows, heads_here, NOPE)
    query_latent = jnp.einsum(
        "qhn,hnl->qhl", nope_part, w_uk, preferred_element_type=jnp.float32
    ).astype(jnp.bfloat16)
    rope_part = query_rope.reshape(shard_rows, heads_here, ROPE)
    own_rows = lax.axis_index("ctx") * shard_rows + jnp.arange(shard_rows, dtype=jnp.int32)
    query_pos = folded_position(own_rows, shard_rows, shard_count)
    initial = (
        jnp.full((shard_rows, heads_here), -1e30, jnp.float32),
        jnp.zeros((shard_rows, heads_here), jnp.float32),
        jnp.zeros((shard_rows, heads_here, latent.shape[1]), jnp.float32),
    )

    def direct_map(row_ids):
        return folded_position(row_ids, shard_rows, shard_count)

    keys_all = lax.all_gather(jnp.concatenate([latent, key_rope], axis=1), "ctx", axis=0, tiled=True)
    fold_keys = make_fold(query_latent, rope_part, query_pos, direct_map, score_scale)
    final_state = fold_keys(
        initial,
        (
            keys_all[:, : latent.shape[1]],
            keys_all[:, latent.shape[1] :],
        ),
        jnp.int32(0),
    )
    best_state, total_state, accum_state = final_state
    latent_out = (accum_state / total_state[:, :, None]).astype(jnp.bfloat16)
    head_out = jnp.einsum(
        "qhl,hlv->qhv", latent_out, w_uv, preferred_element_type=jnp.float32
    ).astype(jnp.bfloat16)
    heads_all = lax.all_gather(head_out.reshape(shard_rows, -1), "ctx", axis=0, tiled=True)
    partial_sum = jnp.einsum(
        "qk,kd->qd",
        heads_all,
        w_out.reshape(-1, w_out.shape[2]),
        preferred_element_type=jnp.float32,
    ).astype(jnp.bfloat16)
    head_count = lax.axis_size("head")
    own_rows = shard_rows // head_count
    by_owner = partial_sum.reshape(shard_count, head_count, own_rows, w_out.shape[2])
    summed = lax.psum_scatter(by_owner, "head", scatter_dimension=1, tiled=True)
    swapped = lax.all_to_all(summed[:, 0], "ctx", split_axis=0, concat_axis=0, tiled=True)
    mixed = swapped.transpose(1, 0, 2).reshape(own_rows, shard_count * w_out.shape[2])
    return mixed


def solution(mesh):
    placed = (
        P("ctx", "head"),
        P("ctx", "head"),
        P("ctx", None),
        P("ctx", None),
        P("head", None, None),
        P("head", None, None),
        P("head", None, "ctx"),
    )
    return jax.shard_map(
        shards, mesh=mesh, in_specs=placed, out_specs=P(("ctx", "head"), None), check_vma=False
    )
```

```python
import functools
import math

import jax
import jax.numpy as jnp
from jax import lax
from jax.experimental import pallas as pl
from jax.experimental.pallas import tpu as pltpu
from jax.sharding import PartitionSpec as P

NOPE = 128
ROPE = 64
GROUPS = 4
KEY_STEP = 256
MESH = pl.DeviceIdType.MESH


def remote(src, dst, send_sem, recv_sem, device):
    return pltpu.make_async_remote_copy(
        src_ref=src,
        dst_ref=dst,
        send_sem=send_sem,
        recv_sem=recv_sem,
        device_id=device,
        device_id_type=MESH,
    )


def each(start, stop, body):
    def step(index, carry):
        body(index)
        return carry

    lax.fori_loop(start, stop, step, 0)


def kernel(
    n_ctx,
    n_head,
    q_ref,
    qr_ref,
    lat_ref,
    kr_ref,
    wuk_hbm,
    wuv_hbm,
    wo_hbm,
    out_ref,
    wuk,
    wuv,
    wo,
    blocks,
    keys,
    queries,
    latent_out,
    heads,
    part_out,
    part_in,
    summed,
    owned,
    load_sem,
    w_send,
    w_recv,
    k_recv,
    k_send_z,
    k_send_y,
    k_send_s,
    h_recv,
    h_send_z,
    h_send_s,
    p_send,
    p_recv,
    o_send,
    o_recv,
):
    rows = lat_ref.shape[0]
    half = rows // 2
    lat_dim = lat_ref.shape[1]
    heads_here = wuk_hbm.shape[0]
    line = n_ctx // 4
    me = lax.axis_index("ctx")
    group = lax.axis_index("head")
    a = me // 4
    b = (me // 2) % 2
    core = me % 2

    def dev(a_at, b_at, core_at):
        return (4 * a_at + 2 * b_at + core_at, group)

    def slot_dev(slot):
        return dev(slot // 2, b, slot % 2)

    slot_me = 2 * a + core
    slots = 2 * line

    load_uk = pltpu.make_async_copy(wuk_hbm, wuk, load_sem.at[0])
    load_uv = pltpu.make_async_copy(wuv_hbm, wuv, load_sem.at[1])
    load_wo = pltpu.make_async_copy(wo_hbm, wo.at[b], load_sem.at[2])
    load_uk.start()
    load_uv.start()
    load_wo.start()

    blocks[me, :, :lat_dim] = lat_ref[...]
    blocks[me, :, lat_dim : lat_dim + ROPE] = kr_ref[...]
    blocks[me, :, lat_dim + ROPE :] = jnp.zeros((rows, 128 - ROPE), jnp.bfloat16)

    barrier = pltpu.get_barrier_semaphore()

    def greet(step):
        other = lax.rem(slot_me + step, slots)
        pl.semaphore_signal(barrier, inc=1, device_id=slot_dev(other), device_id_type=MESH)

    each(1, slots, greet)
    pl.semaphore_signal(barrier, inc=1, device_id=dev(a, 1 - b, core), device_id_type=MESH)
    for step in range(1, n_head):
        pl.semaphore_signal(
            barrier,
            inc=1,
            device_id=(me, lax.rem(group + step, n_head)),
            device_id_type=MESH,
        )
    pl.semaphore_wait(barrier, slots - 1 + 1 + n_head - 1)

    def key_block(src_a, src_b):
        return 4 * src_a + 2 * src_b + core

    def key_copy(index, send_sem, device):
        return remote(blocks.at[index], blocks.at[index], send_sem, k_recv.at[index], device)

    def key_right(src):
        return key_copy(key_block(src, b), k_send_z.at[src], dev(a + 1, b, core))

    def key_left(src, sem):
        return key_copy(key_block(src, b), k_send_z.at[sem], dev(a - 1, b, core))

    def key_y(src):
        return key_copy(key_block(src, b), k_send_y.at[src], dev(a, 1 - b, core))

    def key_s(src, src_b):
        return key_copy(key_block(src, src_b), k_send_s.at[src_b, src], dev(a, b, 1 - core))

    @pl.when(a < line - 1)
    def _():
        key_right(a).start()

    @pl.when(a > 0)
    def _():
        key_left(a, line).start()

    key_y(a).start()
    key_s(a, b).start()

    def relay_keys(k):
        @pl.when(a - k >= 0)
        def _():
            src = a - k
            key_s(src, b).wait_recv()

            @pl.when(a < line - 1)
            def _():
                key_right(src).start()

            key_y(src).start()
            key_s(src, b).start()

        @pl.when(a + k < line)
        def _():
            src = a + k
            key_s(src, b).wait_recv()

            @pl.when(a > 0)
            def _():
                key_left(src, src).start()

            key_y(src).start()
            key_s(src, b).start()

    heads_group = heads_here // GROUPS
    load_uk.wait()
    for g in range(GROUPS):

        def query_pair(p):
            rope = qr_ref[:, pl.ds(pl.multiple_of(p * 2 * ROPE, 2 * ROPE), 2 * ROPE)]
            for odd in range(2):
                h = 2 * p + odd
                q = q_ref[:, pl.ds(pl.multiple_of(h * NOPE, NOPE), NOPE)]
                ql = jnp.dot(q, wuk[h], preferred_element_type=jnp.float32).astype(jnp.bfloat16)
                tail = rope[:, odd * ROPE : (odd + 1) * ROPE]
                tail = jnp.concatenate([tail, jnp.zeros_like(tail)], axis=1)
                for part in range(2):
                    at = pl.ds(pl.multiple_of(h * half, half), half)
                    queries[part, at, :lat_dim] = ql[part * half : (part + 1) * half]
                    queries[part, at, lat_dim:] = tail[part * half : (part + 1) * half]

        each(g * heads_group // 2, (g + 1) * heads_group // 2, query_pair)
        each(
            1 + -(-g * (line - 1) // GROUPS),
            1 + -(-(g + 1) * (line - 1) // GROUPS),
            relay_keys,
        )

    def far_keys(src):
        key_s(src, 1 - b).wait_recv()
        key_s(src, 1 - b).start()

    each(0, line, far_keys)

    depth = wo_hbm.shape[0] // GROUPS

    def weight_copy(g, owner):
        at = pl.ds(pl.multiple_of(g * depth, depth), depth)
        return remote(
            wo_hbm.at[at],
            wo.at[owner, at],
            w_send.at[g],
            w_recv.at[g],
            dev(a, 1 - b, core),
        )

    for g in range(GROUPS):
        weight_copy(g, b).start()

    def near_keys(src):
        for src_b in range(2):
            index = 4 * src + 2 * src_b + (1 - core)
            remote(
                blocks.at[index],
                blocks.at[index],
                k_send_s.at[src_b, src],
                k_recv.at[index],
                dev(a, b, 1 - core),
            ).wait_recv()

    each(0, line, near_keys)

    def place_keys(c):
        low = pl.ds(pl.multiple_of(c * half, half), half)
        high = pl.ds(pl.multiple_of((2 * n_ctx - 1 - c) * half, half), half)
        keys[low] = blocks[c, :half]
        keys[high] = blocks[c, half:]

    each(0, n_ctx, place_keys)

    def head_copy(src_core, src, g, send_sem, device):
        return remote(
            heads.at[src_core, src, g],
            heads.at[src_core, src, g],
            send_sem,
            h_recv.at[src_core, src, g],
            device,
        )

    def head_right(src, g):
        return head_copy(core, src, g, h_send_z.at[src, g], dev(a + 1, b, core))

    def head_left(src, g, sem):
        return head_copy(core, src, g, h_send_z.at[sem, g], dev(a - 1, b, core))

    def head_s(src, g):
        return head_copy(core, src, g, h_send_s.at[src, g], dev(a, b, 1 - core))

    scale = (NOPE + ROPE) ** -0.5 * math.log2(math.e)
    group_rows = heads_group * half
    steps = 2 * n_ctx * half // KEY_STEP

    def attend(g, part, base, count):
        length = count * KEY_STEP
        q = queries[part, pl.ds(pl.multiple_of(g * group_rows, group_rows), group_rows)]
        scores = lax.dot_general(
            q,
            keys[:length],
            (((1,), (1,)), ((), ())),
            preferred_element_type=jnp.float32,
        )
        shape = (group_rows, KEY_STEP)
        row = lax.rem(lax.broadcasted_iota(jnp.int32, shape, 0), half)
        column = lax.broadcasted_iota(jnp.int32, shape, 1)
        visible = column - row <= base - (length - KEY_STEP)
        last = jnp.where(visible, scores[:, length - KEY_STEP :], -jnp.inf)
        if count > 1:
            scores = jnp.concatenate([scores[:, : length - KEY_STEP], last], axis=1)
        else:
            scores = last
        best = jnp.max(scores, axis=1, keepdims=True)
        weights = jnp.exp2((scores - best) * scale)
        total = jnp.sum(weights, axis=1, keepdims=True)
        accum = jnp.dot(
            weights.astype(jnp.bfloat16),
            keys[:length, :lat_dim],
            preferred_element_type=jnp.float32,
        )
        latent_out[part] = (accum / total).astype(jnp.bfloat16)

    load_uv.wait()

    def attend_group(g):
        for part in range(2):
            base = me * half if part == 0 else (2 * n_ctx - 1 - me) * half
            need = base // KEY_STEP + 1
            for count in range(1, steps + 1):
                if (count <= (steps + 1) // 2) if part == 0 else (count >= steps // 2):

                    @pl.when(need == count)
                    def _():
                        attend(g, part, base, count)

        for i in range(heads_group):
            h = g * heads_group + i
            rows_at = slice(i * half, (i + 1) * half)
            lhs = jnp.concatenate([latent_out[0, rows_at], latent_out[1, rows_at]], axis=0)
            head = jnp.dot(lhs, wuv[h], preferred_element_type=jnp.float32)
            heads[core, a, g, :, i * 128 : (i + 1) * 128] = head.astype(jnp.bfloat16)

        @pl.when(a < line - 1)
        def _():
            head_right(a, g).start()

        @pl.when(a > 0)
        def _():
            head_left(a, g, line).start()

        head_s(a, g).start()

    each(0, GROUPS, attend_group)

    def relay_heads(k):
        def one(g):
            @pl.when(a - k >= 0)
            def _():
                src = a - k
                head_s(src, g).wait_recv()

                @pl.when(a < line - 1)
                def _():
                    head_right(src, g).start()

                head_s(src, g).start()

            @pl.when(a + k < line)
            def _():
                src = a + k
                head_s(src, g).wait_recv()

                @pl.when(a > 0)
                def _():
                    head_left(src, g, src).start()

                head_s(src, g).start()

        each(0, GROUPS, one)

    each(1, line, relay_heads)

    def near_heads(src):
        for g in range(GROUPS):
            head_copy(1 - core, src, g, h_send_s.at[src, g], dev(a, b, 1 - core)).wait_recv()

    each(0, line, near_heads)

    own_rows = rows // n_head
    cols = wo.shape[2]

    def part_copy(target, owner):
        return remote(
            part_out.at[target, owner],
            part_in.at[group, owner],
            p_send.at[target, owner],
            p_recv.at[group, owner],
            (me, target),
        )

    def part_arrival(source, owner):
        return remote(
            part_out.at[source, owner],
            part_in.at[source, owner],
            p_send.at[source, owner],
            p_recv.at[source, owner],
            (me, source),
        )

    def project(owner):
        total = jnp.zeros((slots * rows, cols), jnp.float32)
        for g in range(GROUPS):
            lhs = heads[:, :, g].reshape(slots * rows, depth)
            total = total + jnp.dot(
                lhs, wo[owner, g * depth : (g + 1) * depth], preferred_element_type=jnp.float32
            )
        total = total.reshape(slots, rows, cols)
        for target in range(n_head):
            part_out[target, owner] = total[
                :, target * own_rows : (target + 1) * own_rows
            ].astype(jnp.bfloat16)
        for step in range(1, n_head):
            part_copy(lax.rem(group + step, n_head), owner).start()

    load_wo.wait()
    project(b)
    for g in range(GROUPS):
        weight_copy(g, 1 - b).wait_recv()
    project(1 - b)

    for owner in (b, 1 - b):
        total = part_out[group, owner].astype(jnp.float32)
        for step in range(1, n_head):
            source = lax.rem(group + step, n_head)
            part_arrival(source, owner).wait_recv()
            total = total + part_in[source, owner].astype(jnp.float32)
        total = total.astype(jnp.bfloat16)
        for half_core in range(2):
            for at in range(line):
                summed[2 * at + half_core, owner] = total[half_core * line + at]

    def owned_copy(slot):
        return remote(
            summed.at[slot],
            owned.at[slot_me],
            o_send.at[slot],
            o_recv.at[slot_me],
            slot_dev(slot),
        )

    def owned_arrival(slot):
        return remote(
            summed.at[slot],
            owned.at[slot],
            o_send.at[slot],
            o_recv.at[slot],
            slot_dev(slot),
        )

    each(1, slots, lambda step: owned_copy(lax.rem(slot_me + step, slots)).start())
    owned[slot_me] = summed[slot_me]

    def key_sends(src):
        @pl.when(jnp.logical_or(jnp.logical_and(src <= a, a < line - 1), jnp.logical_and(src > a, a > 0)))
        def _():
            key_right(src).wait_send()
            for g in range(GROUPS):
                head_right(src, g).wait_send()

        key_y(src).wait_send()
        for src_b in range(2):
            key_s(src, src_b).wait_send()
        for g in range(GROUPS):
            head_s(src, g).wait_send()

    each(0, line, key_sends)

    @pl.when(a > 0)
    def _():
        key_left(a, line).wait_send()
        for g in range(GROUPS):
            head_left(a, g, line).wait_send()

    for g in range(GROUPS):
        weight_copy(g, b).wait_send()
    for step in range(1, n_head):
        for owner in range(2):
            part_copy(lax.rem(group + step, n_head), owner).wait_send()

    each(1, slots, lambda step: owned_arrival(lax.rem(slot_me + step, slots)).wait_recv())
    each(1, slots, lambda step: owned_copy(lax.rem(slot_me + step, slots)).wait_send())
    out_ref[...] = jnp.concatenate(
        [owned[2 * (c // 4) + c % 2, (c // 2) % 2] for c in range(n_ctx)], axis=1
    )


def shards(q_nope, query_rope, latent, key_rope, w_uk, w_uv, w_out):
    rows, lat_dim = latent.shape
    n_ctx = lax.axis_size("ctx")
    n_head = lax.axis_size("head")
    heads_here = w_uk.shape[0]
    value_dim = w_uv.shape[2]
    cols = w_out.shape[2]
    line = n_ctx // 4
    slots = 2 * line
    own_rows = rows // n_head
    group_width = heads_here // GROUPS * value_dim
    wide = lat_dim + 128
    bf16 = jnp.bfloat16
    dma = pltpu.SemaphoreType.DMA
    vmem = pl.BlockSpec(memory_space=pltpu.VMEM)
    anywhere = pl.BlockSpec(memory_space=pl.ANY)
    return pl.pallas_call(
        functools.partial(kernel, n_ctx, n_head),
        out_shape=jax.ShapeDtypeStruct((own_rows, n_ctx * cols), bf16),
        in_specs=[vmem] * 4 + [anywhere] * 3,
        out_specs=vmem,
        scratch_shapes=[
            pltpu.VMEM(w_uk.shape, bf16),
            pltpu.VMEM(w_uv.shape, bf16),
            pltpu.VMEM((2, heads_here * value_dim, cols), bf16),
            pltpu.VMEM((n_ctx, rows, wide), bf16),
            pltpu.VMEM((n_ctx * rows, wide), bf16),
            pltpu.VMEM((2, heads_here * rows // 2, wide), bf16),
            pltpu.VMEM((2, heads_here // GROUPS * rows // 2, lat_dim), bf16),
            pltpu.VMEM((2, line, GROUPS, rows, group_width), bf16),
            pltpu.VMEM((n_head, 2, slots, own_rows, cols), bf16),
            pltpu.VMEM((n_head, 2, slots, own_rows, cols), bf16),
            pltpu.VMEM((slots, 2, own_rows, cols), bf16),
            pltpu.VMEM((slots, 2, own_rows, cols), bf16),
            dma((3,)),
            dma((GROUPS,)),
            dma((GROUPS,)),
            dma((n_ctx,)),
            dma((line + 1,)),
            dma((line,)),
            dma((2, line)),
            dma((2, line, GROUPS)),
            dma((line + 1, GROUPS)),
            dma((line, GROUPS)),
            dma((n_head, 2)),
            dma((n_head, 2)),
            dma((slots,)),
            dma((slots,)),
        ],
        compiler_params=pltpu.CompilerParams(
            collective_id=0, has_side_effects=True, vmem_limit_bytes=56 * 1024 * 1024
        ),
    )(
        q_nope,
        query_rope,
        latent,
        key_rope,
        w_uk,
        w_uv,
        w_out.reshape(heads_here * value_dim, cols),
    )


def solution(mesh):
    placed = (
        P("ctx", "head"),
        P("ctx", "head"),
        P("ctx", None),
        P("ctx", None),
        P("head", None, None),
        P("head", None, None),
        P("head", None, "ctx"),
    )
    return jax.shard_map(
        shards, mesh=mesh, in_specs=placed, out_specs=P(("ctx", "head"), None), check_vma=False
    )
```

```python
import functools
import math

import jax
import jax.numpy as jnp
from jax import lax
from jax.experimental import pallas as pl
from jax.experimental.pallas import tpu as pltpu
from jax.sharding import PartitionSpec as P

NOPE = 128
ROPE = 64
GROUPS = 4
CHUNKS = 8
KEY_STEP = 256
MESH = pl.DeviceIdType.MESH


def remote(src, dst, send_sem, recv_sem, device):
    return pltpu.make_async_remote_copy(
        src_ref=src,
        dst_ref=dst,
        send_sem=send_sem,
        recv_sem=recv_sem,
        device_id=device,
        device_id_type=MESH,
    )


def each(start, stop, body):
    def step(index, carry):
        body(index)
        return carry

    lax.fori_loop(start, stop, step, 0)


def kernel(
    n_ctx,
    n_head,
    q_ref,
    qr_ref,
    lat_ref,
    kr_ref,
    wuk_hbm,
    wuv_hbm,
    wo_hbm,
    out_ref,
    wuk,
    wuv,
    wt,
    wo,
    blocks,
    keys,
    queries,
    latent_out,
    heads,
    part_out,
    part_in,
    summed,
    owned,
    load_sem,
    w_send,
    w_recv,
    k_recv,
    k_send_z,
    k_send_y,
    k_send_s,
    h_recv,
    h_send_z,
    h_send_s,
    p_send,
    p_recv,
    o_send,
    o_recv,
):
    rows = lat_ref.shape[0]
    half = rows // 2
    lat_dim = lat_ref.shape[1]
    heads_here = wuk_hbm.shape[0]
    line = n_ctx // 4
    me = lax.axis_index("ctx")
    group = lax.axis_index("head")
    a = me // 4
    b = (me // 2) % 2
    core = me % 2

    def dev(a_at, b_at, core_at):
        return (4 * a_at + 2 * b_at + core_at, group)

    def slot_dev(slot):
        return dev(slot // 2, b, slot % 2)

    slot_me = 2 * a + core
    slots = 2 * line

    load_uk = pltpu.make_async_copy(wuk_hbm, wuk, load_sem.at[0])
    load_uv = pltpu.make_async_copy(wuv_hbm, wuv, load_sem.at[1])
    load_wo = pltpu.make_async_copy(wo_hbm, wt.at[b], load_sem.at[2])
    load_uk.start()
    load_uv.start()
    load_wo.start()

    blocks[me, :, :lat_dim] = lat_ref[...]
    blocks[me, :, lat_dim : lat_dim + ROPE] = kr_ref[...]
    blocks[me, :, lat_dim + ROPE :] = jnp.zeros((rows, 128 - ROPE), jnp.bfloat16)

    barrier = pltpu.get_barrier_semaphore()

    def greet(step):
        other = lax.rem(slot_me + step, slots)
        pl.semaphore_signal(barrier, inc=1, device_id=slot_dev(other), device_id_type=MESH)

    each(1, slots, greet)
    pl.semaphore_signal(barrier, inc=1, device_id=dev(a, 1 - b, core), device_id_type=MESH)
    for step in range(1, n_head):
        pl.semaphore_signal(
            barrier,
            inc=1,
            device_id=(me, lax.rem(group + step, n_head)),
            device_id_type=MESH,
        )
    pl.semaphore_wait(barrier, slots - 1 + 1 + n_head - 1)

    def key_block(src_a, src_b):
        return 4 * src_a + 2 * src_b + core

    def key_copy(index, send_sem, device):
        return remote(blocks.at[index], blocks.at[index], send_sem, k_recv.at[index], device)

    def key_right(src):
        return key_copy(key_block(src, b), k_send_z.at[src], dev(a + 1, b, core))

    def key_left(src, sem):
        return key_copy(key_block(src, b), k_send_z.at[sem], dev(a - 1, b, core))

    def key_y(src):
        return key_copy(key_block(src, b), k_send_y.at[src], dev(a, 1 - b, core))

    def key_s(src, src_b):
        return key_copy(key_block(src, src_b), k_send_s.at[src_b, src], dev(a, b, 1 - core))

    @pl.when(a < line - 1)
    def _():
        key_right(a).start()

    @pl.when(a > 0)
    def _():
        key_left(a, line).start()

    key_y(a).start()
    key_s(a, b).start()

    depth = heads_here // CHUNKS

    def weight_copy(chunk, owner):
        at = pl.ds(chunk * depth, depth)
        return remote(
            wo_hbm.at[at],
            wt.at[owner, at],
            w_send.at[chunk],
            w_recv.at[chunk],
            dev(a, 1 - b, core),
        )

    weight_copy(0, b).start()

    def relay_keys(k):
        @pl.when(a - k >= 0)
        def _():
            src = a - k
            key_s(src, b).wait_recv()

            @pl.when(a < line - 1)
            def _():
                key_right(src).start()

            key_y(src).start()
            key_s(src, b).start()

        @pl.when(a + k < line)
        def _():
            src = a + k
            key_s(src, b).wait_recv()

            @pl.when(a > 0)
            def _():
                key_left(src, src).start()

            key_y(src).start()
            key_s(src, b).start()

    heads_group = heads_here // GROUPS
    load_uk.wait()
    for g in range(GROUPS):

        def query_pair(p):
            rope = qr_ref[:, pl.ds(pl.multiple_of(p * 2 * ROPE, 2 * ROPE), 2 * ROPE)]
            for odd in range(2):
                h = 2 * p + odd
                q = q_ref[:, pl.ds(pl.multiple_of(h * NOPE, NOPE), NOPE)]
                ql = jnp.dot(q, wuk[h], preferred_element_type=jnp.float32).astype(jnp.bfloat16)
                tail = rope[:, odd * ROPE : (odd + 1) * ROPE]
                tail = jnp.concatenate([tail, jnp.zeros_like(tail)], axis=1)
                for part in range(2):
                    at = pl.ds(pl.multiple_of(h * half, half), half)
                    queries[part, at, :lat_dim] = ql[part * half : (part + 1) * half]
                    queries[part, at, lat_dim:] = tail[part * half : (part + 1) * half]

        each(g * heads_group // 2, (g + 1) * heads_group // 2, query_pair)
        each(
            1 + -(-g * (line - 1) // GROUPS),
            1 + -(-(g + 1) * (line - 1) // GROUPS),
            relay_keys,
        )

    each(1, CHUNKS, lambda chunk: weight_copy(chunk, b).start())

    def far_keys(src):
        key_s(src, 1 - b).wait_recv()
        key_s(src, 1 - b).start()

    each(0, line, far_keys)

    def near_keys(src):
        for src_b in range(2):
            index = 4 * src + 2 * src_b + (1 - core)
            remote(
                blocks.at[index],
                blocks.at[index],
                k_send_s.at[src_b, src],
                k_recv.at[index],
                dev(a, b, 1 - core),
            ).wait_recv()

    value_dim = wt.shape[3]

    def turn(owner):
        def one(h):
            wo[owner, pl.ds(pl.multiple_of(h * value_dim, value_dim), value_dim)] = wt[owner, h].T

        each(0, heads_here, one)

    load_wo.wait()
    turn(b)
    each(0, line, near_keys)

    def place_keys(c):
        low = pl.ds(pl.multiple_of(c * half, half), half)
        high = pl.ds(pl.multiple_of((2 * n_ctx - 1 - c) * half, half), half)
        keys[low] = blocks[c, :half]
        keys[high] = blocks[c, half:]

    each(0, n_ctx, place_keys)

    def head_copy(src_core, src, g, send_sem, device):
        return remote(
            heads.at[src_core, src, g],
            heads.at[src_core, src, g],
            send_sem,
            h_recv.at[src_core, src, g],
            device,
        )

    def head_right(src, g):
        return head_copy(core, src, g, h_send_z.at[src, g], dev(a + 1, b, core))

    def head_left(src, g, sem):
        return head_copy(core, src, g, h_send_z.at[sem, g], dev(a - 1, b, core))

    def head_s(src, g):
        return head_copy(core, src, g, h_send_s.at[src, g], dev(a, b, 1 - core))

    scale = (NOPE + ROPE) ** -0.5 * math.log2(math.e)
    group_rows = heads_group * half
    steps = 2 * n_ctx * half // KEY_STEP

    def attend(g, part, base, count):
        length = count * KEY_STEP
        q = queries[part, pl.ds(pl.multiple_of(g * group_rows, group_rows), group_rows)]
        scores = lax.dot_general(
            q,
            keys[:length],
            (((1,), (1,)), ((), ())),
            preferred_element_type=jnp.float32,
        )
        shape = (group_rows, KEY_STEP)
        row = lax.rem(lax.broadcasted_iota(jnp.int32, shape, 0), half)
        column = lax.broadcasted_iota(jnp.int32, shape, 1)
        visible = column - row <= base - (length - KEY_STEP)
        last = jnp.where(visible, scores[:, length - KEY_STEP :], -jnp.inf)
        if count > 1:
            scores = jnp.concatenate([scores[:, : length - KEY_STEP], last], axis=1)
        else:
            scores = last
        best = jnp.max(scores, axis=1, keepdims=True)
        weights = jnp.exp2((scores - best) * scale)
        total = jnp.sum(weights, axis=1, keepdims=True)
        accum = jnp.dot(
            weights.astype(jnp.bfloat16),
            keys[:length, :lat_dim],
            preferred_element_type=jnp.float32,
        )
        latent_out[part] = (accum / total).astype(jnp.bfloat16)

    load_uv.wait()

    def attend_group(g):
        for part in range(2):
            base = me * half if part == 0 else (2 * n_ctx - 1 - me) * half
            need = base // KEY_STEP + 1
            for count in range(1, steps + 1):
                if (count <= (steps + 1) // 2) if part == 0 else (count >= steps // 2):

                    @pl.when(need == count)
                    def _():
                        attend(g, part, base, count)

        for i in range(heads_group):
            h = g * heads_group + i
            rows_at = slice(i * half, (i + 1) * half)
            lhs = jnp.concatenate([latent_out[0, rows_at], latent_out[1, rows_at]], axis=0)
            head = jnp.dot(lhs, wuv[h], preferred_element_type=jnp.float32)
            heads[core, a, g, :, i * 128 : (i + 1) * 128] = head.astype(jnp.bfloat16)

        @pl.when(a < line - 1)
        def _():
            head_right(a, g).start()

        @pl.when(a > 0)
        def _():
            head_left(a, g, line).start()

        head_s(a, g).start()

    each(0, GROUPS, attend_group)

    def relay_heads(k):
        def one(g):
            @pl.when(a - k >= 0)
            def _():
                src = a - k
                head_s(src, g).wait_recv()

                @pl.when(a < line - 1)
                def _():
                    head_right(src, g).start()

                head_s(src, g).start()

            @pl.when(a + k < line)
            def _():
                src = a + k
                head_s(src, g).wait_recv()

                @pl.when(a > 0)
                def _():
                    head_left(src, g, src).start()

                head_s(src, g).start()

        each(0, GROUPS, one)

    own_rows = rows // n_head
    cols = wo.shape[2]
    width = heads_group * value_dim

    def sides(k, body):
        @pl.when(a - k >= 0)
        def _():
            body(a - k)

        @pl.when(jnp.logical_and(k >= 1, a + k < line))
        def _():
            body(a + k)

    def part_copy(target, owner, src):
        return remote(
            part_out.at[target, owner, src],
            part_in.at[group, owner, src],
            p_send.at[target, owner, src],
            p_recv.at[group, owner, src],
            (me, target),
        )

    def part_arrival(source, owner, src):
        return remote(
            part_out.at[source, owner, src],
            part_in.at[source, owner, src],
            p_send.at[source, owner, src],
            p_recv.at[source, owner, src],
            (me, source),
        )

    def near_heads(src):
        for g in range(GROUPS):
            head_copy(1 - core, src, g, h_send_s.at[src, g], dev(a, b, 1 - core)).wait_recv()

    def project(src, owner):
        total = jnp.zeros((2 * rows, cols), jnp.float32)
        for g in range(GROUPS):
            lhs = heads[:, src, g].reshape(2 * rows, width)
            total = total + jnp.dot(
                lhs, wo[owner, g * width : (g + 1) * width], preferred_element_type=jnp.float32
            )
        total = total.reshape(2, rows, cols)
        for target in range(n_head):
            part_out[target, owner, src] = total[
                :, target * own_rows : (target + 1) * own_rows
            ].astype(jnp.bfloat16)
        for step in range(1, n_head):
            part_copy(lax.rem(group + step, n_head), owner, src).start()

    def owned_copy(slot, owner):
        return remote(
            summed.at[slot, owner],
            owned.at[slot_me, owner],
            o_send.at[slot, owner],
            o_recv.at[slot_me, owner],
            slot_dev(slot),
        )

    def owned_arrival(slot, owner):
        return remote(
            summed.at[slot, owner],
            owned.at[slot, owner],
            o_send.at[slot, owner],
            o_recv.at[slot, owner],
            slot_dev(slot),
        )

    def finish(src, owner):
        total = part_out[group, owner, src].astype(jnp.float32)
        for step in range(1, n_head):
            source = lax.rem(group + step, n_head)
            part_arrival(source, owner, src).wait_recv()
            total = total + part_in[source, owner, src].astype(jnp.float32)
        total = total.astype(jnp.bfloat16)
        for at in range(2):
            slot = 2 * src + at
            summed[slot, owner] = total[at]

            @pl.when(slot != slot_me)
            def _():
                owned_copy(slot, owner).start()

            @pl.when(slot == slot_me)
            def _():
                owned[slot_me, owner] = total[at]

    def arrive_own(src):
        near_heads(src)
        project(src, b)

    def far_step(k):
        sides(k, lambda src: project(src, 1 - b))

    def far_finish(k):
        sides(k, lambda src: finish(src, 1 - b))

    def near_step(k):
        relay_heads(k + 1)
        sides(k, arrive_own)

        @pl.when(k >= 1)
        def _():
            sides(k - 1, lambda src: finish(src, b))

    each(0, line - 2, near_step)
    sides(line - 2, arrive_own)
    sides(line - 3, lambda src: finish(src, b))
    each(0, CHUNKS, lambda chunk: weight_copy(chunk, 1 - b).wait_recv())
    turn(1 - b)
    each(0, line - 1, far_step)
    sides(line - 2, lambda src: finish(src, b))
    each(0, line - 1, far_finish)
    relay_heads(line - 1)

    def arrive_last(src):
        near_heads(src)
        project(src, b)
        project(src, 1 - b)

    def finish_last(src):
        finish(src, b)
        finish(src, 1 - b)

    sides(line - 1, arrive_last)
    sides(line - 1, finish_last)

    def key_sends(src):
        @pl.when(jnp.logical_or(jnp.logical_and(src <= a, a < line - 1), jnp.logical_and(src > a, a > 0)))
        def _():
            key_right(src).wait_send()
            for g in range(GROUPS):
                head_right(src, g).wait_send()

        key_y(src).wait_send()
        for src_b in range(2):
            key_s(src, src_b).wait_send()
        for g in range(GROUPS):
            head_s(src, g).wait_send()

    each(0, line, key_sends)

    @pl.when(a > 0)
    def _():
        key_left(a, line).wait_send()
        for g in range(GROUPS):
            head_left(a, g, line).wait_send()

    each(0, CHUNKS, lambda chunk: weight_copy(chunk, b).wait_send())

    def part_sends(src):
        for step in range(1, n_head):
            for owner in range(2):
                part_copy(lax.rem(group + step, n_head), owner, src).wait_send()

    each(0, line, part_sends)

    def owned_waits(step):
        for owner in range(2):
            owned_arrival(lax.rem(slot_me + step, slots), owner).wait_recv()
            owned_copy(lax.rem(slot_me + step, slots), owner).wait_send()

    each(1, slots, owned_waits)
    out_ref[...] = jnp.concatenate(
        [owned[2 * (c // 4) + c % 2, (c // 2) % 2] for c in range(n_ctx)], axis=1
    )


def shards(q_nope, query_rope, latent, key_rope, w_uk, w_uv, w_out):
    rows, lat_dim = latent.shape
    n_ctx = lax.axis_size("ctx")
    n_head = lax.axis_size("head")
    heads_here = w_uk.shape[0]
    value_dim = w_uv.shape[2]
    cols = w_out.shape[2]
    line = n_ctx // 4
    slots = 2 * line
    own_rows = rows // n_head
    group_width = heads_here // GROUPS * value_dim
    wide = lat_dim + 128
    bf16 = jnp.bfloat16
    dma = pltpu.SemaphoreType.DMA
    vmem = pl.BlockSpec(memory_space=pltpu.VMEM)
    anywhere = pl.BlockSpec(memory_space=pl.ANY)
    return pl.pallas_call(
        functools.partial(kernel, n_ctx, n_head),
        out_shape=jax.ShapeDtypeStruct((own_rows, n_ctx * cols), bf16),
        in_specs=[vmem] * 4 + [anywhere] * 3,
        out_specs=vmem,
        scratch_shapes=[
            pltpu.VMEM(w_uk.shape, bf16),
            pltpu.VMEM(w_uv.shape, bf16),
            pltpu.VMEM((2, heads_here, cols, value_dim), bf16),
            pltpu.VMEM((2, heads_here * value_dim, cols), bf16),
            pltpu.VMEM((n_ctx, rows, wide), bf16),
            pltpu.VMEM((n_ctx * rows, wide), bf16),
            pltpu.VMEM((2, heads_here * rows // 2, wide), bf16),
            pltpu.VMEM((2, heads_here // GROUPS * rows // 2, lat_dim), bf16),
            pltpu.VMEM((2, line, GROUPS, rows, group_width), bf16),
            pltpu.VMEM((n_head, 2, line, 2, own_rows, cols), bf16),
            pltpu.VMEM((n_head, 2, line, 2, own_rows, cols), bf16),
            pltpu.VMEM((slots, 2, own_rows, cols), bf16),
            pltpu.VMEM((slots, 2, own_rows, cols), bf16),
            dma((3,)),
            dma((CHUNKS,)),
            dma((CHUNKS,)),
            dma((n_ctx,)),
            dma((line + 1,)),
            dma((line,)),
            dma((2, line)),
            dma((2, line, GROUPS)),
            dma((line + 1, GROUPS)),
            dma((line, GROUPS)),
            dma((n_head, 2, line)),
            dma((n_head, 2, line)),
            dma((slots, 2)),
            dma((slots, 2)),
        ],
        compiler_params=pltpu.CompilerParams(
            collective_id=0, has_side_effects=True, vmem_limit_bytes=56 * 1024 * 1024
        ),
    )(
        q_nope,
        query_rope,
        latent,
        key_rope,
        w_uk,
        w_uv,
        w_out.transpose(0, 2, 1),
    )


def solution(mesh):
    placed = (
        P("ctx", "head"),
        P("ctx", "head"),
        P("ctx", None),
        P("ctx", None),
        P("head", None, None),
        P("head", None, None),
        P("head", None, "ctx"),
    )
    return jax.shard_map(
        shards, mesh=mesh, in_specs=placed, out_specs=P(("ctx", "head"), None), check_vma=False
    )
```
